32 devices in a mesh: groups: 2 (over x), sink: 16 (over z, y, core).
Axes of the slice: x: 2, y: 2, z: 4, core: 2. Of those that a mesh axis runs over, the one named last changes fastest.
Arguments:
- blocks: bfloat16 [4096, 128, 128], P(('groups', 'sink')), parts along dimension 0, may hold values from -6 to 6
- peram: bfloat16 [256, 4, 16, 128], P(('groups', 'sink')), parts along dimension 0, may hold values from -0.5 to 0.5
- src_blocks: bfloat16 [256, 2, 128, 128], P(('groups', 'sink')), parts along dimension 0, may hold values from -1 to 1
- sink_spin: int32 [16, 3], replicated, may hold values from 0 to 3
- src_spin: int32 [1, 3], replicated, may hold values from 0 to 3
- pairs: int32 [4, 2], replicated, may hold values from 0 to 3
Outputs:
- transformed: bfloat16 [256, 16, 128, 128], P(('groups', 'sink')), parts along dimension 0
- correlator: float32 [2, 4, 4], P('groups'), parts along dimension 0
The draws below stay inside these ranges and needn't reach their ends.
There are 2 independent parts, one for each index of `groups`. The reference program is written for one: setup_inputs(seed, part) draws one part's arguments, and reference() takes and returns one part's arrays. A program takes and returns all parts, laid end to end along the dimension named above; an argument that names none is the same for every part. Nothing has to cross between parts.
All inputs are finite; a program needn't handle non-finite values.
Results may differ from the reference program's by a relative error of at most 0.0087.
Values may be sent and summed in bfloat16 or wider, within the bound.
No kernel may reach another device: no remote copies, remote signals or barrier semaphores. Data moves between devices by JAX's collectives and lax.ppermute only.
A program may use at most 64 MiB of HBM per device.

```python
import jax
import jax.numpy as jnp
from jax import lax

NEV = 128
NMOM = 4
NC = 2
NPAIR = 4
TSRC = 1
NBLK = 16
TSNK = 4


def draw_src_blocks(key, part):
    key = jax.random.fold_in(key, 7)
    keys = jax.random.split(key, 4)
    total_rows = TSRC * NEV
    shape = (total_rows, NC, NEV, NEV)
    rise = jnp.power(3.0, jnp.arange(total_rows).astype(jnp.float32) / total_rows)
    row_scale = jnp.power(10.0, jax.random.uniform(keys[0], (total_rows,), jnp.float32)) * rise
    col_scale = jnp.power(10.0, jax.random.uniform(keys[1], (NEV,), jnp.float32))
    base = jnp.clip(jax.random.normal(keys[3], shape, jnp.float32), -6.0, 6.0)
    values = base * row_scale[:, None, None, None] * col_scale[None, None, None, :]
    return (values / (NEV ** 1.5 * 25.0)).astype(jnp.bfloat16)


def with_ends(result, own_key, least, largest):
    place = [jax.random.randint(jax.random.fold_in(own_key, axis), (), 0, length) for axis, length in enumerate(result.shape)]
    widest = result.shape.index(max(result.shape))
    next_to = place[:widest] + [(place[widest] + 1) % result.shape[widest]] + place[widest + 1:]
    return result.at[tuple(place)].set(least).at[tuple(next_to)].set(largest)


def levels(key, shape, cuts, low, largest):
    def one(dim, blocks):
        heights = jax.random.uniform(jax.random.fold_in(jax.random.fold_in(key, 6), dim), (blocks,), jnp.float32, low / len(cuts), largest / len(cuts))
        return jnp.repeat(jnp.exp(heights), shape[dim] // blocks).reshape((-1,) + (1,) * (len(shape) - dim - 1))

    level = one(*cuts[0])
    for cut in cuts[1:]:
        level = level * one(*cut)
    return level


def bell_draw(own_key, dims, scale, reach, shards=(), kind=jnp.bfloat16):
    entries = scale * jax.random.normal(own_key, dims, jnp.float32)
    if shards:
        entries = entries * levels(own_key, dims, shards, -0.22, 0.18)
    return jnp.clip(entries, -reach, reach).astype(kind)


def setup_inputs(seed: int = 0, part: int = 0) -> dict:
    seeds = jax.random.split(jax.random.key(seed), 7)
    part_splits = jax.random.split(jax.random.fold_in(seeds[6], part), 7)
    return {
        "blocks": bell_draw(part_splits[0], (NBLK * NEV, NEV, NEV), 1.0, 6.0, ((0, 16),)),
        "peram": bell_draw(part_splits[1], (TSRC * NEV, TSNK, 16, NEV), NEV ** -0.5, 0.5, ((0, 16),)),
        "src_blocks": draw_src_blocks(jax.random.fold_in(jax.random.fold_in(seeds[6], part), 71), part),
        "sink_spin": with_ends(jax.random.randint(seeds[3], (NBLK, 3), 0, 4), jax.random.fold_in(seeds[3], 1), 0, 3).astype(jnp.int32),
        "src_spin": jax.random.randint(seeds[4], (TSRC, 3), 0, 4).astype(jnp.int32),
        "pairs": with_ends(jax.random.randint(seeds[5], (NPAIR, 2), 0, NMOM), jax.random.fold_in(seeds[5], 1), 0, NMOM - 1).astype(jnp.int32),
    }


def reference(blocks, peram, src_blocks, sink_spin, src_spin, pairs):
    cubes = blocks.reshape(NBLK, NEV, NEV, NEV)
    tables = peram.reshape(TSRC, NEV, TSNK, 16, NEV)
    sources = src_blocks.reshape(TSRC, NEV, NC, NEV, NEV).astype(jnp.float32)

    def one_block(index):
        cube = cubes[index]
        time_of = index // NMOM
        spins = sink_spin[index]
        outs_list = []
        correlations = []
        for source in range(TSRC):
            codes = 4 * spins + src_spin[source]
            fac_i = tables[source, :, time_of, codes[0], :]
            fac_j = tables[source, :, time_of, codes[1], :]
            fac_k = tables[source, :, time_of, codes[2], :]
            first = jnp.dot(cube.reshape(NEV * NEV, NEV), fac_k, preferred_element_type=jnp.float32)
            first = first.reshape(NEV, NEV, NEV).astype(jnp.bfloat16)
            second = jnp.einsum("ijk,jJ->iJk", first.astype(jnp.float32), fac_j.astype(jnp.float32)).astype(jnp.bfloat16)
            third = jnp.einsum("iI,iJk->IJk", fac_i.astype(jnp.float32), second.astype(jnp.float32)).astype(jnp.bfloat16)
            outs_list.append(third)
            correlations.append(jnp.einsum("ijk,icjk->c", third.astype(jnp.float32), sources[source]))
        return jnp.stack(outs_list), jnp.stack(correlations)

    moved, correlation = lax.map(one_block, jnp.arange(NBLK, dtype=jnp.int32))
    transformed = jnp.transpose(moved, (1, 2, 0, 3, 4)).reshape(TSRC * NEV, NBLK, NEV, NEV)
    grid = jnp.transpose(correlation, (1, 0, 2)).reshape(TSRC, TSNK, NMOM, NC)
    first_one = grid[:, :, pairs[:, 0], :]
    second_one = grid[:, :, pairs[:, 1], :]
    correlator = first_one[..., 0] * second_one[..., 1] - first_one[..., 1] * second_one[..., 0]
    return transformed, correlator
```

```python
import jax
import jax.numpy as jnp
from jax import lax
from jax.experimental import pallas as pl
from jax.experimental.pallas import tpu as pltpu
from jax.sharding import PartitionSpec as P

NMOM = 4
PITCH = 136
GROUP = 16
F32 = jnp.float32
BF16 = jnp.bfloat16
IN_VMEM = pl.BlockSpec(memory_space=pltpu.VMEM)
IN_SMEM = pl.BlockSpec(memory_space=pltpu.SMEM)
IN_HBM = pl.BlockSpec(memory_space=pltpu.HBM)
AHEAD = 5


def in_hbm(array):
    return pltpu.with_memory_space_constraint(array, pltpu.HBM)


def in_vmem(array):
    return pltpu.with_memory_space_constraint(array, pltpu.VMEM)


def dot(left, right):
    return jnp.dot(left, right, preferred_element_type=F32)


def pick_kernel(sink_spin, src_spin, peram, out, table):
    times, codes = peram.shape[1:3]
    for t in range(times):
        table[pl.ds(t * codes, codes)] = jnp.swapaxes(peram[:, t].astype(F32), 0, 1)
    for b in range(out.shape[0]):
        for m in range(3):
            code = (b // NMOM) * codes + 4 * sink_spin[m, b] + src_spin[0, m]
            out[b, m] = table[code].astype(BF16)


def pick(peram, sink_spin, src_spin):
    rows, times, codes, width = peram.shape
    blocks = sink_spin.shape[0]
    return pl.pallas_call(
        pick_kernel,
        out_shape=jax.ShapeDtypeStruct((blocks, 3, rows, width), BF16),
        in_specs=[IN_SMEM, IN_SMEM, IN_VMEM],
        out_specs=IN_VMEM,
        scratch_shapes=[pltpu.VMEM((times * codes, rows, width), F32)],
        name="pick",
    )(sink_spin.T, src_spin, peram)


def contract(me, blocks, factors, classes):
    width = blocks.shape[0]
    rows = factors.shape[2]
    half = width // 2
    steps = half // GROUP

    def kernel(me, blocks, factors, *refs):
        outs, (left0, wide2, second, held, kept, sems) = refs[: len(classes)], refs[len(classes) :]
        made = [kept.at[q - AHEAD] if q >= AHEAD else out for q, out in enumerate(outs)]
        copies = []
        for step in range(steps):
            part = pl.ds(step * 2 * GROUP, 2 * GROUP)
            copies.append(pltpu.make_async_copy(blocks.at[part], held.at[part], sems.at[step]))
            copies[-1].start()
        parts = [factors[:, m].astype(F32).reshape(width, width) for m in range(3)]
        left1 = parts[1].T.astype(BF16)
        left0[...] = parts[0].T
        zero = jnp.zeros((width, width), BF16)
        right2 = parts[2].astype(BF16)
        wide2[...] = jnp.concatenate(
            [jnp.concatenate([right2, zero], 1), jnp.concatenate([zero, right2], 1)], 0
        )

        for step in range(steps):
            copies[step].wait()
            base = step * 2 * GROUP
            pairs = [
                jnp.concatenate([held[base + 2 * q], held[base + 2 * q + 1]], 1)
                for q in range(GROUP)
            ]
            first = dot(jnp.concatenate(pairs, 0), wide2[...]).astype(BF16)
            for q in range(GROUP):
                done = dot(left1, first[q * width : (q + 1) * width]).astype(BF16).astype(F32)
                for h in range(2):
                    start = (base + 2 * q + h) * PITCH
                    second[pl.ds(start, width), :] = done[:, h * width : (h + 1) * width]
        left = jnp.concatenate(
            [left0[pl.ds(pl.multiple_of((me[0] ^ d) * rows, rows), rows), :] for d in classes], 0
        ).astype(BF16)

        for step in range(steps):
            base = step * 2 * GROUP
            done = []
            for q in range(GROUP):
                right = jnp.concatenate(
                    [
                        second[pl.ds(base + 2 * q + h, width, stride=PITCH), :].astype(BF16)
                        for h in range(2)
                    ],
                    1,
                )
                done.append(dot(left, right))
            for index in range(len(classes)):
                tiles = []
                for q in range(GROUP):
                    own = done[q][index * rows : (index + 1) * rows]
                    tiles += [own[:, :width], own[:, width:]]
                part = pl.ds(base * rows, 2 * GROUP * rows)
                made[index][part, :] = jnp.concatenate(tiles, 0).astype(BF16)
            for index in range(AHEAD, len(classes)):
                copies.append(
                    pltpu.make_async_copy(
                        made[index].at[part], outs[index].at[part], sems.at[len(copies)]
                    )
                )
                copies[-1].start()
        for copy in copies[steps:]:
            copy.wait()

    flops = 2 * 3 * width**4
    return pl.pallas_call(
        kernel,
        out_shape=[pltpu.VMEM((width * rows, width), BF16)] * AHEAD
        + [pltpu.HBM((width * rows, width), BF16)] * (len(classes) - AHEAD),
        in_specs=[IN_SMEM, IN_HBM, IN_VMEM],
        out_specs=[IN_VMEM] * AHEAD + [IN_HBM] * (len(classes) - AHEAD),
        scratch_shapes=[
            pltpu.VMEM((width, width), F32),
            pltpu.VMEM((2 * width, 2 * width), BF16),
            pltpu.VMEM((width * PITCH, width), F32),
            pltpu.VMEM(blocks.shape, BF16),
            pltpu.VMEM((len(classes) - AHEAD, width * rows, width), BF16),
            pltpu.SemaphoreType.DMA((steps * (1 + len(classes) - AHEAD),)),
        ],
        compiler_params=pltpu.CompilerParams(vmem_limit_bytes=40 * 2**20),
        cost_estimate=pl.CostEstimate(
            flops=flops, bytes_accessed=4 * width**3, transcendentals=0
        ),
        name="contract",
    )(me, in_hbm(blocks), factors)


def receive(block, message, src, out, sums, following):
    rows, ncount, width, _ = src.shape
    blocks = lax.axis_size("sink")
    operands = [block, in_vmem(message), in_vmem(src)]
    specs = [IN_SMEM, IN_VMEM, IN_VMEM]
    shapes = [
        pltpu.HBM((rows, blocks, width, width), BF16),
        pltpu.VMEM((blocks, ncount, width), F32),
    ]
    places = [IN_HBM, IN_VMEM]
    aliases = {}
    if out is not None:
        aliases.update({3: 0, 4: 1})
        operands += [in_hbm(out), in_vmem(sums)]
        specs += places
    if following is not None:
        aliases[len(operands)] = 2
        operands.append(in_hbm(following))
        specs.append(IN_HBM)
        shapes.append(pltpu.HBM(following.shape, following.dtype))
        places = places + [IN_HBM]

    def kernel(*refs):
        block, message, src = refs[:3]
        out, sums = refs[len(operands) : len(operands) + 2]
        wide, stage, sems = refs[-3:]
        if 4 in aliases:
            sums[...] = refs[4][...]
        index = block[0]
        wide[...] = message[...].astype(F32)
        stores = []
        for r in range(rows):
            stage[r] = wide[pl.ds(r, width, stride=rows), :].astype(BF16)
            stores.append(pltpu.make_async_copy(stage.at[r], out.at[r, index], sems.at[r]))
            stores[-1].start()
        for c in range(ncount):
            total = jnp.zeros((8, width), F32)
            for r in range(rows):
                product = stage[r].astype(F32) * src[r, c].astype(F32)
                total = total + jnp.sum(product.reshape(width // 8, 8, width), axis=0)
            sums[index, pl.ds(c, 1)] = jnp.sum(total, axis=0, keepdims=True)
        for store in stores:
            store.wait()

    results = pl.pallas_call(
        kernel,
        out_shape=shapes,
        in_specs=specs,
        out_specs=places,
        scratch_shapes=[
            pltpu.VMEM((rows * width, width), F32),
            pltpu.VMEM((rows, width, width), BF16),
            pltpu.SemaphoreType.DMA((rows,)),
        ],
        input_output_aliases=aliases,
        cost_estimate=pl.CostEstimate(flops=0, bytes_accessed=0, transcendentals=0),
        name="receive",
    )(*operands)
    return results if following is not None else (*results, None)


def determinant(correlation, pairs, tsources):
    ncount = correlation.shape[-1]
    grid = correlation.reshape(tsources, -1, NMOM, ncount)
    momenta = jnp.arange(NMOM, dtype=jnp.int32)
    pick_first = (pairs[:, 0][:, None] == momenta[None, :]).astype(F32)
    pick_second = (pairs[:, 1][:, None] == momenta[None, :]).astype(F32)
    first_one = jnp.einsum("pm,stmc->stpc", pick_first, grid, precision=lax.Precision.HIGHEST)
    second_one = jnp.einsum("pm,stmc->stpc", pick_second, grid, precision=lax.Precision.HIGHEST)
    return first_one[..., 0] * second_one[..., 1] - first_one[..., 1] * second_one[..., 0]


def by_classes(blocks, peram, src_blocks, sink_spin, src_spin, pairs):
    devices = lax.axis_size("sink")
    position = lax.axis_index("sink").astype(jnp.int32)
    picked = pick(peram, sink_spin, src_spin)
    factors = lax.all_to_all(picked, "sink", split_axis=0, concat_axis=0, tiled=True)
    far = list(range(devices // 2, devices))
    near = list(range(devices // 2 - 1, 0, -1))
    far = [d for pair in zip(far[: len(far) // 2], far[len(far) // 2 :]) for d in pair]
    order = []
    for f, c in zip(far, near + [0]):
        order += [f, c]
    order = order[:-2] + order[:-3:-1]
    sent = [d for d in order if d]
    messages = dict(zip(order, contract(position.reshape(1), blocks, factors, order)))

    def send(d, message):
        return lax.ppermute(message, "sink", [(i, i ^ d) for i in range(devices)])

    come = {d: send(d, messages[d]) for d in sent[:AHEAD]}
    come[0] = messages[0]
    out = sums = None
    for step, d in enumerate(order):
        ahead = sent[step + AHEAD] if step + AHEAD < len(sent) else None
        out, sums, following = receive(
            (position ^ d).reshape(1),
            come[d],
            src_blocks,
            out,
            sums,
            None if ahead is None else messages[ahead],
        )
        if ahead is not None:
            come[ahead] = send(ahead, following)
    shift = 1
    while shift < devices:
        sums = sums + send(shift, sums)
        shift *= 2
    correlation = jnp.sum(sums, axis=-1)
    return out, determinant(correlation, pairs, 1)


def by_all_to_all(blocks, peram, src_blocks, sink_spin, src_spin, pairs):
    width = blocks.shape[1]
    tsources = src_spin.shape[0]
    devices = lax.axis_size("sink")
    position = lax.axis_index("sink")
    per_rows = peram.shape[0]
    own_source = (position * per_rows + jnp.arange(per_rows, dtype=jnp.int32)) // width
    target_time = jnp.arange(devices, dtype=jnp.int32) // NMOM
    codes = 4 * sink_spin[None, :, :] + src_spin[own_source][:, None, :]
    picked = peram[
        jnp.arange(per_rows, dtype=jnp.int32)[:, None, None], target_time[None, :, None], codes, :
    ]
    incoming = lax.all_to_all(picked, "sink", split_axis=1, concat_axis=0, tiled=True)
    factors = incoming.reshape(tsources, width, 3, width)

    def transform(source):
        first = dot(blocks.reshape(-1, width), factors[source, :, 2]).astype(BF16)
        second = jnp.einsum(
            "ijk,jJ->iJk",
            first.reshape(blocks.shape),
            factors[source, :, 1],
            preferred_element_type=F32,
        ).astype(BF16)
        return jnp.einsum(
            "iI,iJk->IJk", factors[source, :, 0], second, preferred_element_type=F32
        ).astype(BF16)

    sending = jnp.stack([transform(s) for s in range(tsources)])
    sending = sending.reshape(tsources * width, 1, width, width)
    regrouped = lax.all_to_all(sending, "sink", split_axis=0, concat_axis=1, tiled=True)
    out_rows = regrouped.shape[0]
    row_source = (position * out_rows + jnp.arange(out_rows, dtype=jnp.int32)) // width
    sums = jnp.einsum("rbjk,rcjk->rbc", regrouped, src_blocks, preferred_element_type=F32)
    selector = (row_source[:, None] == jnp.arange(tsources, dtype=jnp.int32)[None, :]).astype(F32)
    local = jnp.einsum("rs,rbc->sbc", selector, sums, precision=lax.Precision.HIGHEST)
    return regrouped, determinant(lax.psum(local, "sink"), pairs, tsources)


def body(blocks, peram, src_blocks, sink_spin, src_spin, pairs):
    devices = lax.axis_size("sink")
    rows = src_blocks.shape[0]
    small = devices in (8, 16, 32) and src_spin.shape[0] == 1 and rows % 8 == 0
    run = by_classes if small else by_all_to_all
    return run(blocks, peram, src_blocks, sink_spin, src_spin, pairs)


def solution(mesh):
    placed = (
        P(("groups", "sink"), None, None),
        P(("groups", "sink"), None, None, None),
        P(("groups", "sink"), None, None, None),
        P(),
        P(),
        P(),
    )
    return jax.shard_map(
        body,
        mesh=mesh,
        in_specs=placed,
        out_specs=(P(("groups", "sink"), None, None, None), P("groups", None, None)),
        check_vma=False,
    )
```

```python
import jax
import jax.numpy as jnp
from jax import lax
from jax.experimental import pallas as pl
from jax.experimental.pallas import tpu as pltpu
from jax.sharding import PartitionSpec as P

NMOM = 4
PITCH = 136
GROUP = 16
F32 = jnp.float32
BF16 = jnp.bfloat16
IN_VMEM = pl.BlockSpec(memory_space=pltpu.VMEM)
IN_SMEM = pl.BlockSpec(memory_space=pltpu.SMEM)
IN_HBM = pl.BlockSpec(memory_space=pltpu.HBM)
AHEAD = 5
DEPTH = 4


def in_hbm(array):
    return pltpu.with_memory_space_constraint(array, pltpu.HBM)


def in_vmem(array):
    return pltpu.with_memory_space_constraint(array, pltpu.VMEM)


def dot(left, right):
    return jnp.dot(left, right, preferred_element_type=F32)


def pick_kernel(sink_spin, src_spin, peram, out, table):
    times, codes = peram.shape[1:3]
    for t in range(times):
        table[pl.ds(t * codes, codes)] = jnp.swapaxes(peram[:, t].astype(F32), 0, 1)
    for b in range(out.shape[0]):
        for m in range(3):
            code = (b // NMOM) * codes + 4 * sink_spin[m, b] + src_spin[0, m]
            out[b, m] = table[code].astype(BF16)


def pick(peram, sink_spin, src_spin):
    rows, times, codes, width = peram.shape
    blocks = sink_spin.shape[0]
    return pl.pallas_call(
        pick_kernel,
        out_shape=pltpu.VMEM((blocks, 3, rows, width), BF16),
        in_specs=[IN_SMEM, IN_SMEM, IN_VMEM],
        out_specs=IN_VMEM,
        scratch_shapes=[pltpu.VMEM((times * codes, rows, width), F32)],
        name="pick",
    )(sink_spin.T, src_spin, peram)


def left_rows(me, left0, classes, rows):
    parts = [left0[pl.ds(pl.multiple_of((me ^ d) * rows, rows), rows), :] for d in classes]
    return jnp.concatenate(parts, 0).astype(BF16)


def put_tiles(outs, done, base, rows, width):
    for index, out in enumerate(outs):
        tiles = []
        for product in done:
            own = product[index * rows : (index + 1) * rows]
            tiles += [own[:, :width], own[:, width:]]
        out[pl.ds(base * rows, len(tiles) * rows), :] = jnp.concatenate(tiles, 0).astype(BF16)


def contract(blocks, factors, classes, place):
    width = blocks.shape[0]
    rows = factors.shape[2]
    steps = width // 2 // GROUP
    count = len(classes)
    shape = (width * rows, width)
    stored = place is not pltpu.VMEM

    def kernel(blocks, factors, *refs):
        me = lax.axis_index("sink")
        outs, (held, left0, wide2, second, sems) = refs[:count], refs[count : count + 5]
        made = refs[count + 5 :] if stored else outs
        loads, stores = [], []
        for step in range(steps):
            part = pl.ds(step * 2 * GROUP, 2 * GROUP)
            loads.append(pltpu.make_async_copy(blocks.at[part], held.at[part], sems.at[step]))
        for step in range(DEPTH):
            loads[step].start()
        parts = [factors[:, m].astype(F32).reshape(width, width) for m in range(3)]
        left1 = parts[1].T.astype(BF16)
        left0[...] = parts[0].T
        zero = jnp.zeros((width, width), BF16)
        right2 = parts[2].astype(BF16)
        wide2[...] = jnp.concatenate(
            [jnp.concatenate([right2, zero], 1), jnp.concatenate([zero, right2], 1)], 0
        )
        for step in range(steps):
            loads[step].wait()
            if step + DEPTH < steps:
                loads[step + DEPTH].start()
            base = step * 2 * GROUP
            pairs = [
                jnp.concatenate([held[base + 2 * q], held[base + 2 * q + 1]], 1)
                for q in range(GROUP)
            ]
            first = dot(jnp.concatenate(pairs, 0), wide2[...]).astype(BF16)
            for q in range(GROUP):
                done = dot(left1, first[q * width : (q + 1) * width]).astype(BF16).astype(F32)
                for h in range(2):
                    start = (base + 2 * q + h) * PITCH
                    second[pl.ds(start, width), :] = done[:, h * width : (h + 1) * width]
        left = left_rows(me, left0, classes, rows)
        for step in range(steps):
            base = step * 2 * GROUP
            done = []
            for q in range(GROUP):
                halves = [
                    second[pl.ds(base + 2 * q + h, width, stride=PITCH), :].astype(BF16)
                    for h in range(2)
                ]
                done.append(dot(left, jnp.concatenate(halves, 1)))
            put_tiles(made, done, base, rows, width)
            part = pl.ds(base * rows, 2 * GROUP * rows)
            for index in range(count if stored else 0):
                sem = sems.at[steps + step * count + index]
                stores.append(
                    pltpu.make_async_copy(made[index].at[part], outs[index].at[part], sem)
                )
                stores[-1].start()
        for store in stores:
            store.wait()

    return pl.pallas_call(
        kernel,
        out_shape=[place(shape, BF16)] * count,
        in_specs=[IN_HBM, IN_VMEM],
        out_specs=[IN_HBM if stored else IN_VMEM] * count,
        scratch_shapes=[
            pltpu.VMEM(blocks.shape, BF16),
            pltpu.VMEM((width, width), F32),
            pltpu.VMEM((2 * width, 2 * width), BF16),
            pltpu.VMEM((width * PITCH, width), F32),
            pltpu.SemaphoreType.DMA((steps * (1 + count) + 1,)),
        ]
        + [pltpu.VMEM(shape, BF16)] * (count if stored else 0),
        compiler_params=pltpu.CompilerParams(vmem_limit_bytes=40 * 2**20),
        cost_estimate=pl.CostEstimate(flops=0, bytes_accessed=0, transcendentals=0),
        name="contract",
    )(in_hbm(blocks), in_vmem(factors))


def receive(d, message, src, out, sums, following):
    rows, ncount, width, _ = src.shape
    blocks = lax.axis_size("sink")
    operands = [in_vmem(message), in_vmem(src)]
    specs = [IN_VMEM, IN_VMEM]
    shapes = [
        pltpu.HBM((rows, blocks, width, width), BF16),
        pltpu.VMEM((blocks, ncount, width), F32),
    ]
    places = [IN_HBM, IN_VMEM]
    aliases = {}
    if out is not None:
        aliases.update({2: 0, 3: 1})
        operands += [in_hbm(out), in_vmem(sums)]
        specs += places
    if following is not None:
        aliases[len(operands)] = 2
        operands.append(in_hbm(following))
        specs.append(IN_HBM)
        shapes.append(pltpu.HBM(following.shape, following.dtype))
        places = places + [IN_HBM]

    def kernel(*refs):
        message, src = refs[:2]
        out, sums = refs[len(operands) : len(operands) + 2]
        wide, stage, sems = refs[-3:]
        if 3 in aliases:
            sums[...] = refs[3][...]
        index = lax.axis_index("sink") ^ d
        wide[...] = message[...].astype(F32)
        stores = []
        for r in range(rows):
            stage[r] = wide[pl.ds(r, width, stride=rows), :].astype(BF16)
            stores.append(pltpu.make_async_copy(stage.at[r], out.at[r, index], sems.at[r]))
            stores[-1].start()
        for c in range(ncount):
            total = jnp.zeros((8, width), F32)
            for r in range(rows):
                product = stage[r].astype(F32) * src[r, c].astype(F32)
                total = total + jnp.sum(product.reshape(width // 8, 8, width), axis=0)
            sums[index, pl.ds(c, 1)] = jnp.sum(total, axis=0, keepdims=True)
        for store in stores:
            store.wait()

    results = pl.pallas_call(
        kernel,
        out_shape=shapes,
        in_specs=specs,
        out_specs=places,
        scratch_shapes=[
            pltpu.VMEM((rows * width, width), F32),
            pltpu.VMEM((rows, width, width), BF16),
            pltpu.SemaphoreType.DMA((rows,)),
        ],
        input_output_aliases=aliases,
        cost_estimate=pl.CostEstimate(flops=0, bytes_accessed=0, transcendentals=0),
        name="receive",
    )(*operands)
    return results if following is not None else (*results, None)


def determinant(correlation, pairs, tsources):
    ncount = correlation.shape[-1]
    grid = correlation.reshape(tsources, -1, NMOM, ncount)
    momenta = jnp.arange(NMOM, dtype=jnp.int32)
    pick_first = (pairs[:, 0][:, None] == momenta[None, :]).astype(F32)
    pick_second = (pairs[:, 1][:, None] == momenta[None, :]).astype(F32)
    first_one = jnp.einsum("pm,stmc->stpc", pick_first, grid, precision=lax.Precision.HIGHEST)
    second_one = jnp.einsum("pm,stmc->stpc", pick_second, grid, precision=lax.Precision.HIGHEST)
    return first_one[..., 0] * second_one[..., 1] - first_one[..., 1] * second_one[..., 0]


def finish(sums, pairs):
    devices, _, width = sums.shape
    times = devices // NMOM

    def kernel(pairs, sums, out):
        row = jnp.sum(sums[...], axis=0)
        time = lax.broadcasted_iota(jnp.int32, (times, width), 0)
        lane = lax.broadcasted_iota(jnp.int32, (times, width), 1)
        columns = []
        for p in range(pairs.shape[1]):
            values = [
                jnp.sum(
                    jnp.where(lane == 2 * (NMOM * time + pairs[k, p]) + c, row, 0.0),
                    axis=1,
                    keepdims=True,
                )
                for k in range(2)
                for c in range(2)
            ]
            columns.append(values[0] * values[3] - values[1] * values[2])
        out[0] = jnp.concatenate(columns, 1)

    return pl.pallas_call(
        kernel,
        out_shape=jax.ShapeDtypeStruct((1, times, pairs.shape[0]), F32),
        in_specs=[IN_SMEM, IN_VMEM],
        out_specs=IN_VMEM,
        name="finish",
    )(pairs.T, sums)


def by_classes(blocks, peram, src_blocks, sink_spin, src_spin, pairs):
    devices = lax.axis_size("sink")
    rows, ncount, width, _ = src_blocks.shape

    def send(d, message):
        return lax.ppermute(message, "sink", [(i, i ^ d) for i in range(devices)])

    picked = pick(peram, sink_spin, src_spin)
    factors = lax.all_to_all(picked, "sink", split_axis=0, concat_axis=0, tiled=True)
    far = list(range(devices // 2, devices))
    near = list(range(devices // 2 - 1, 0, -1))
    far = [d for pair in zip(far[: len(far) // 2], far[len(far) // 2 :]) for d in pair]
    sent = []
    for f, c in zip(far, near + [None]):
        sent += [f] if c is None else [f, c]
    early = contract(blocks, factors, sent[:AHEAD], pltpu.VMEM)
    come = {d: send(d, message) for d, message in zip(sent, early)}
    rest = sent[AHEAD:] + [0]
    messages = dict(zip(rest, contract(blocks, factors, rest, pltpu.HBM)))
    out, sums, _ = receive(0, messages[0], src_blocks, None, None, None)
    for step, d in enumerate(sent):
        ahead = sent[step + AHEAD] if step + AHEAD < len(sent) else None
        out, sums, following = receive(
            d,
            come[d],
            src_blocks,
            out,
            sums,
            None if ahead is None else messages[ahead],
        )
        if ahead is not None:
            come[ahead] = send(ahead, following)
    row = jnp.sum(sums, axis=-1).reshape(1, 1, devices * ncount)
    row = jnp.pad(row, ((0, 0), (0, 0), (0, width - devices * ncount)))
    rows_of_all = lax.all_to_all(
        jnp.broadcast_to(row, (devices, 1, width)), "sink", split_axis=0, concat_axis=0, tiled=True
    )
    return out, finish(rows_of_all, pairs)


def by_all_to_all(blocks, peram, src_blocks, sink_spin, src_spin, pairs):
    width = blocks.shape[1]
    tsources = src_spin.shape[0]
    devices = lax.axis_size("sink")
    position = lax.axis_index("sink")
    per_rows = peram.shape[0]
    own_source = (position * per_rows + jnp.arange(per_rows, dtype=jnp.int32)) // width
    target_time = jnp.arange(devices, dtype=jnp.int32) // NMOM
    codes = 4 * sink_spin[None, :, :] + src_spin[own_source][:, None, :]
    picked = peram[
        jnp.arange(per_rows, dtype=jnp.int32)[:, None, None], target_time[None, :, None], codes, :
    ]
    incoming = lax.all_to_all(picked, "sink", split_axis=1, concat_axis=0, tiled=True)
    factors = incoming.reshape(tsources, width, 3, width)

    def transform(source):
        first = dot(blocks.reshape(-1, width), factors[source, :, 2]).astype(BF16)
        second = jnp.einsum(
            "ijk,jJ->iJk",
            first.reshape(blocks.shape),
            factors[source, :, 1],
            preferred_element_type=F32,
        ).astype(BF16)
        return jnp.einsum(
            "iI,iJk->IJk", factors[source, :, 0], second, preferred_element_type=F32
        ).astype(BF16)

    sending = jnp.stack([transform(s) for s in range(tsources)])
    sending = sending.reshape(tsources * width, 1, width, width)
    regrouped = lax.all_to_all(sending, "sink", split_axis=0, concat_axis=1, tiled=True)
    out_rows = regrouped.shape[0]
    row_source = (position * out_rows + jnp.arange(out_rows, dtype=jnp.int32)) // width
    sums = jnp.einsum("rbjk,rcjk->rbc", regrouped, src_blocks, preferred_element_type=F32)
    selector = (row_source[:, None] == jnp.arange(tsources, dtype=jnp.int32)[None, :]).astype(F32)
    local = jnp.einsum("rs,rbc->sbc", selector, sums, precision=lax.Precision.HIGHEST)
    return regrouped, determinant(lax.psum(local, "sink"), pairs, tsources)


def body(blocks, peram, src_blocks, sink_spin, src_spin, pairs):
    devices = lax.axis_size("sink")
    small = devices == 16 and src_spin.shape[0] == 1 and src_blocks.shape[:2] == (8, 2)
    run = by_classes if small else by_all_to_all
    return run(blocks, peram, src_blocks, sink_spin, src_spin, pairs)


def solution(mesh):
    placed = (
        P(("groups", "sink"), None, None),
        P(("groups", "sink"), None, None, None),
        P(("groups", "sink"), None, None, None),
        P(),
        P(),
        P(),
    )
    return jax.shard_map(
        body,
        mesh=mesh,
        in_specs=placed,
        out_specs=(P(("groups", "sink"), None, None, None), P("groups", None, None)),
        check_vma=False,
    )
```

```python
import jax
import jax.numpy as jnp
from jax import lax
from jax.experimental import pallas as pl
from jax.experimental.pallas import tpu as pltpu
from jax.sharding import PartitionSpec as P

NMOM = 4
PITCH = 136
GROUP = 32
F32 = jnp.float32
BF16 = jnp.bfloat16
IN_VMEM = pl.BlockSpec(memory_space=pltpu.VMEM)
IN_SMEM = pl.BlockSpec(memory_space=pltpu.SMEM)
IN_HBM = pl.BlockSpec(memory_space=pltpu.HBM)
AHEAD = 5
DEPTH = 2


def in_hbm(array):
    return pltpu.with_memory_space_constraint(array, pltpu.HBM)


def in_vmem(array):
    return pltpu.with_memory_space_constraint(array, pltpu.VMEM)


def dot(left, right):
    return jnp.dot(left, right, preferred_element_type=F32)


def pick_kernel(sink_spin, src_spin, peram, out, table):
    times, codes = peram.shape[1:3]
    for t in range(times):
        table[pl.ds(t * codes, codes)] = jnp.swapaxes(peram[:, t].astype(F32), 0, 1)
    for b in range(out.shape[0]):
        for m in range(3):
            code = (b // NMOM) * codes + 4 * sink_spin[m, b] + src_spin[0, m]
            out[b, m] = table[code].astype(BF16)


def pick(peram, sink_spin, src_spin):
    rows, times, codes, width = peram.shape
    blocks = sink_spin.shape[0]
    return pl.pallas_call(
        pick_kernel,
        out_shape=pltpu.VMEM((blocks, 3, rows, width), BF16),
        in_specs=[IN_SMEM, IN_SMEM, IN_VMEM],
        out_specs=IN_VMEM,
        scratch_shapes=[pltpu.VMEM((times * codes, rows, width), F32)],
        name="pick",
    )(sink_spin.T, src_spin, peram)


def left_rows(me, left0, classes, rows):
    parts = [left0[pl.ds(pl.multiple_of((me ^ d) * rows, rows), rows), :] for d in classes]
    return jnp.concatenate(parts, 0).astype(BF16)


def put_tiles(outs, done, base, rows, width):
    for index, out in enumerate(outs):
        tiles = []
        for product in done:
            own = product[index * rows : (index + 1) * rows]
            tiles += [own[:, :width], own[:, width:]]
        out[pl.ds(base * rows, len(tiles) * rows), :] = jnp.concatenate(tiles, 0).astype(BF16)


def contract(blocks, factors, classes, place):
    width = blocks.shape[0]
    rows = factors.shape[2]
    steps = width // 2 // GROUP
    count = len(classes)
    shape = (width * rows, width)
    stored = place is not pltpu.VMEM

    def kernel(blocks, factors, *refs):
        me = lax.axis_index("sink")
        outs, (held, left0, wide2, second, sems) = refs[:count], refs[count : count + 5]
        made = refs[count + 5 :] if stored else outs
        loads, stores = [], []
        for step in range(steps):
            part = pl.ds(step * 2 * GROUP, 2 * GROUP)
            loads.append(pltpu.make_async_copy(blocks.at[part], held.at[part], sems.at[step]))
        for step in range(DEPTH):
            loads[step].start()
        parts = [factors[:, m].astype(F32).reshape(width, width) for m in range(3)]
        left1 = parts[1].T.astype(BF16)
        left0[...] = parts[0].T
        zero = jnp.zeros((width, width), BF16)
        right2 = parts[2].astype(BF16)
        wide2[...] = jnp.concatenate(
            [jnp.concatenate([right2, zero], 1), jnp.concatenate([zero, right2], 1)], 0
        )
        for step in range(steps):
            loads[step].wait()
            if step + DEPTH < steps:
                loads[step + DEPTH].start()
            base = step * 2 * GROUP
            pairs = [
                jnp.concatenate([held[base + 2 * q], held[base + 2 * q + 1]], 1)
                for q in range(GROUP)
            ]
            first = dot(jnp.concatenate(pairs, 0), wide2[...]).astype(BF16)
            for q in range(GROUP):
                done = dot(left1, first[q * width : (q + 1) * width]).astype(BF16).astype(F32)
                for h in range(2):
                    start = (base + 2 * q + h) * PITCH
                    second[pl.ds(start, width), :] = done[:, h * width : (h + 1) * width]
        left = left_rows(me, left0, classes, rows)
        for step in range(steps):
            base = step * 2 * GROUP
            done = []
            for q in range(GROUP):
                halves = [
                    second[pl.ds(base + 2 * q + h, width, stride=PITCH), :].astype(BF16)
                    for h in range(2)
                ]
                done.append(dot(left, jnp.concatenate(halves, 1)))
            put_tiles(made, done, base, rows, width)
            part = pl.ds(base * rows, 2 * GROUP * rows)
            for index in range(count if stored else 0):
                sem = sems.at[steps + step * count + index]
                stores.append(
                    pltpu.make_async_copy(made[index].at[part], outs[index].at[part], sem)
                )
                stores[-1].start()
        for store in stores:
            store.wait()

    return pl.pallas_call(
        kernel,
        out_shape=[place(shape, BF16)] * count,
        in_specs=[IN_HBM, IN_VMEM],
        out_specs=[IN_HBM if stored else IN_VMEM] * count,
        scratch_shapes=[
            pltpu.VMEM(blocks.shape, BF16),
            pltpu.VMEM((width, width), F32),
            pltpu.VMEM((2 * width, 2 * width), BF16),
            pltpu.VMEM((width * PITCH, width), F32),
            pltpu.SemaphoreType.DMA((steps * (1 + count) + 1,)),
        ]
        + [pltpu.VMEM(shape, BF16)] * (count if stored else 0),
        compiler_params=pltpu.CompilerParams(vmem_limit_bytes=40 * 2**20),
        cost_estimate=pl.CostEstimate(flops=0, bytes_accessed=0, transcendentals=0),
        name="contract",
    )(in_hbm(blocks), in_vmem(factors))


def receive(d, message, src, out, sums, following):
    rows, ncount, width, _ = src.shape
    blocks = lax.axis_size("sink")
    operands = [in_vmem(message), in_vmem(src)]
    specs = [IN_VMEM, IN_VMEM]
    shapes = [
        pltpu.HBM((rows, blocks, width, width), BF16),
        pltpu.VMEM((blocks, ncount, width), F32),
    ]
    places = [IN_HBM, IN_VMEM]
    aliases = {}
    if out is not None:
        aliases.update({2: 0, 3: 1})
        operands += [in_hbm(out), in_vmem(sums)]
        specs += places
    if following is not None:
        aliases[len(operands)] = 2
        operands.append(in_hbm(following))
        specs.append(IN_HBM)
        shapes.append(pltpu.HBM(following.shape, following.dtype))
        places = places + [IN_HBM]

    def kernel(*refs):
        message, src = refs[:2]
        out, sums = refs[len(operands) : len(operands) + 2]
        wide, stage, sems = refs[-3:]
        if 3 in aliases:
            sums[...] = refs[3][...]
        index = lax.axis_index("sink") ^ d
        wide[...] = message[...].astype(F32)
        stores = []
        for r in range(rows):
            stage[r] = wide[pl.ds(r, width, stride=rows), :].astype(BF16)
            stores.append(pltpu.make_async_copy(stage.at[r], out.at[r, index], sems.at[r]))
            stores[-1].start()
        for c in range(ncount):
            total = jnp.zeros((8, width), F32)
            for r in range(rows):
                product = stage[r].astype(F32) * src[r, c].astype(F32)
                total = total + jnp.sum(product.reshape(width // 8, 8, width), axis=0)
            sums[index, pl.ds(c, 1)] = jnp.sum(total, axis=0, keepdims=True)
        for store in stores:
            store.wait()

    results = pl.pallas_call(
        kernel,
        out_shape=shapes,
        in_specs=specs,
        out_specs=places,
        scratch_shapes=[
            pltpu.VMEM((rows * width, width), F32),
            pltpu.VMEM((rows, width, width), BF16),
            pltpu.SemaphoreType.DMA((rows,)),
        ],
        input_output_aliases=aliases,
        cost_estimate=pl.CostEstimate(flops=0, bytes_accessed=0, transcendentals=0),
        name="receive",
    )(*operands)
    return results if following is not None else (*results, None)


def determinant(correlation, pairs, tsources):
    ncount = correlation.shape[-1]
    grid = correlation.reshape(tsources, -1, NMOM, ncount)
    momenta = jnp.arange(NMOM, dtype=jnp.int32)
    pick_first = (pairs[:, 0][:, None] == momenta[None, :]).astype(F32)
    pick_second = (pairs[:, 1][:, None] == momenta[None, :]).astype(F32)
    first_one = jnp.einsum("pm,stmc->stpc", pick_first, grid, precision=lax.Precision.HIGHEST)
    second_one = jnp.einsum("pm,stmc->stpc", pick_second, grid, precision=lax.Precision.HIGHEST)
    return first_one[..., 0] * second_one[..., 1] - first_one[..., 1] * second_one[..., 0]


def finish(sums, pairs):
    devices, _, width = sums.shape
    times = devices // NMOM

    def kernel(pairs, sums, out):
        row = jnp.sum(sums[...], axis=0)
        time = lax.broadcasted_iota(jnp.int32, (times, width), 0)
        lane = lax.broadcasted_iota(jnp.int32, (times, width), 1)
        columns = []
        for p in range(pairs.shape[1]):
            values = [
                jnp.sum(
                    jnp.where(lane == 2 * (NMOM * time + pairs[k, p]) + c, row, 0.0),
                    axis=1,
                    keepdims=True,
                )
                for k in range(2)
                for c in range(2)
            ]
            columns.append(values[0] * values[3] - values[1] * values[2])
        out[0] = jnp.concatenate(columns, 1)

    return pl.pallas_call(
        kernel,
        out_shape=jax.ShapeDtypeStruct((1, times, pairs.shape[0]), F32),
        in_specs=[IN_SMEM, IN_VMEM],
        out_specs=IN_VMEM,
        name="finish",
    )(pairs.T, sums)


def by_classes(blocks, peram, src_blocks, sink_spin, src_spin, pairs):
    devices = lax.axis_size("sink")
    rows, ncount, width, _ = src_blocks.shape

    def send(d, message):
        return lax.ppermute(message, "sink", [(i, i ^ d) for i in range(devices)])

    picked = pick(peram, sink_spin, src_spin)
    factors = lax.all_to_all(picked, "sink", split_axis=0, concat_axis=0, tiled=True)
    far = list(range(devices // 2, devices))
    near = list(range(devices // 2 - 1, 0, -1))
    far = [d for pair in zip(far[: len(far) // 2], far[len(far) // 2 :]) for d in pair]
    far[:2] = far[1::-1]
    sent = []
    for f, c in zip(far, near + [None]):
        sent += [f] if c is None else [f, c]
    early = contract(blocks, factors, sent[:AHEAD], pltpu.VMEM)
    come = {d: send(d, message) for d, message in zip(sent, early)}
    rest = sent[AHEAD:] + [0]
    messages = dict(zip(rest, contract(blocks, factors, rest, pltpu.HBM)))
    out, sums, _ = receive(0, messages[0], src_blocks, None, None, None)
    for step, d in enumerate(sent):
        ahead = sent[step + AHEAD] if step + AHEAD < len(sent) else None
        out, sums, following = receive(
            d,
            come[d],
            src_blocks,
            out,
            sums,
            None if ahead is None else messages[ahead],
        )
        if ahead is not None:
            come[ahead] = send(ahead, following)
    row = jnp.sum(sums, axis=-1).reshape(1, 1, devices * ncount)
    row = jnp.pad(row, ((0, 0), (0, 0), (0, width - devices * ncount)))
    rows_of_all = lax.all_to_all(
        jnp.broadcast_to(row, (devices, 1, width)), "sink", split_axis=0, concat_axis=0, tiled=True
    )
    return out, finish(rows_of_all, pairs)


def by_all_to_all(blocks, peram, src_blocks, sink_spin, src_spin, pairs):
    width = blocks.shape[1]
    tsources = src_spin.shape[0]
    devices = lax.axis_size("sink")
    position = lax.axis_index("sink")
    per_rows = peram.shape[0]
    own_source = (position * per_rows + jnp.arange(per_rows, dtype=jnp.int32)) // width
    target_time = jnp.arange(devices, dtype=jnp.int32) // NMOM
    codes = 4 * sink_spin[None, :, :] + src_spin[own_source][:, None, :]
    picked = peram[
        jnp.arange(per_rows, dtype=jnp.int32)[:, None, None], target_time[None, :, None], codes, :
    ]
    incoming = lax.all_to_all(picked, "sink", split_axis=1, concat_axis=0, tiled=True)
    factors = incoming.reshape(tsources, width, 3, width)

    def transform(source):
        first = dot(blocks.reshape(-1, width), factors[source, :, 2]).astype(BF16)
        second = jnp.einsum(
            "ijk,jJ->iJk",
            first.reshape(blocks.shape),
            factors[source, :, 1],
            preferred_element_type=F32,
        ).astype(BF16)
        return jnp.einsum(
            "iI,iJk->IJk", factors[source, :, 0], second, preferred_element_type=F32
        ).astype(BF16)

    sending = jnp.stack([transform(s) for s in range(tsources)])
    sending = sending.reshape(tsources * width, 1, width, width)
    regrouped = lax.all_to_all(sending, "sink", split_axis=0, concat_axis=1, tiled=True)
    out_rows = regrouped.shape[0]
    row_source = (position * out_rows + jnp.arange(out_rows, dtype=jnp.int32)) // width
    sums = jnp.einsum("rbjk,rcjk->rbc", regrouped, src_blocks, preferred_element_type=F32)
    selector = (row_source[:, None] == jnp.arange(tsources, dtype=jnp.int32)[None, :]).astype(F32)
    local = jnp.einsum("rs,rbc->sbc", selector, sums, precision=lax.Precision.HIGHEST)
    return regrouped, determinant(lax.psum(local, "sink"), pairs, tsources)


def body(blocks, peram, src_blocks, sink_spin, src_spin, pairs):
    devices = lax.axis_size("sink")
    small = devices == 16 and src_spin.shape[0] == 1 and src_blocks.shape[:2] == (8, 2)
    run = by_classes if small else by_all_to_all
    return run(blocks, peram, src_blocks, sink_spin, src_spin, pairs)


def solution(mesh):
    placed = (
        P(("groups", "sink"), None, None),
        P(("groups", "sink"), None, None, None),
        P(("groups", "sink"), None, None, None),
        P(),
        P(),
        P(),
    )
    return jax.shard_map(
        body,
        mesh=mesh,
        in_specs=placed,
        out_specs=(P(("groups", "sink"), None, None, None), P("groups", None, None)),
        check_vma=False,
    )
```

```python
import jax
import jax.numpy as jnp
from jax import lax
from jax.experimental import pallas as pl
from jax.experimental.pallas import tpu as pltpu
from jax.sharding import PartitionSpec as P

NMOM = 4
PITCH = 136
GROUP = 32
F32 = jnp.float32
BF16 = jnp.bfloat16
IN_VMEM = pl.BlockSpec(memory_space=pltpu.VMEM)
IN_SMEM = pl.BlockSpec(memory_space=pltpu.SMEM)
IN_HBM = pl.BlockSpec(memory_space=pltpu.HBM)
AHEAD = 5
DEPTH = 2


def in_hbm(array):
    return pltpu.with_memory_space_constraint(array, pltpu.HBM)


def in_vmem(array):
    return pltpu.with_memory_space_constraint(array, pltpu.VMEM)


def dot(left, right):
    return jnp.dot(left, right, preferred_element_type=F32)


def pick_kernel(sink_spin, src_spin, peram, out, table):
    times, codes = peram.shape[1:3]
    for t in range(times):
        table[pl.ds(t * codes, codes)] = jnp.swapaxes(peram[:, t].astype(F32), 0, 1)
    for b in range(out.shape[0]):
        for m in range(3):
            code = (b // NMOM) * codes + 4 * sink_spin[m, b] + src_spin[0, m]
            out[b, m] = table[code].astype(BF16)


def pick(peram, sink_spin, src_spin):
    rows, times, codes, width = peram.shape
    blocks = sink_spin.shape[0]
    return pl.pallas_call(
        pick_kernel,
        out_shape=pltpu.VMEM((blocks, 3, rows, width), BF16),
        in_specs=[IN_SMEM, IN_SMEM, IN_VMEM],
        out_specs=IN_VMEM,
        scratch_shapes=[pltpu.VMEM((times * codes, rows, width), F32)],
        name="pick",
    )(sink_spin.T, src_spin, peram)


def left_rows(me, left0, classes, rows):
    parts = [left0[pl.ds(pl.multiple_of((me ^ d) * rows, rows), rows), :] for d in classes]
    return jnp.concatenate(parts, 0).astype(BF16)


def put_tiles(outs, done, base, rows, width):
    for index, out in enumerate(outs):
        tiles = []
        for product in done:
            own = product[index * rows : (index + 1) * rows]
            tiles += [own[:, :width], own[:, width:]]
        out[pl.ds(base * rows, len(tiles) * rows), :] = jnp.concatenate(tiles, 0).astype(BF16)


def contract(blocks, factors, classes, place):
    width = blocks.shape[0]
    rows = factors.shape[2]
    steps = width // 2 // GROUP
    count = len(classes)
    shape = (width * rows, width)
    stored = place is not pltpu.VMEM

    def kernel(blocks, factors, *refs):
        me = lax.axis_index("sink")
        outs, (held, left0, wide2, second, sems) = refs[:count], refs[count : count + 5]
        made = refs[count + 5 :] if stored else outs
        loads, stores = [], []
        for step in range(steps):
            part = pl.ds(step * 2 * GROUP, 2 * GROUP)
            loads.append(pltpu.make_async_copy(blocks.at[part], held.at[part], sems.at[step]))
        for step in range(DEPTH):
            loads[step].start()
        parts = [factors[:, m].astype(F32).reshape(width, width) for m in range(3)]
        left1 = parts[1].T.astype(BF16)
        left0[...] = parts[0].T
        zero = jnp.zeros((width, width), BF16)
        right2 = parts[2].astype(BF16)
        wide2[...] = jnp.concatenate(
            [jnp.concatenate([right2, zero], 1), jnp.concatenate([zero, right2], 1)], 0
        )
        for step in range(steps):
            loads[step].wait()
            if step + DEPTH < steps:
                loads[step + DEPTH].start()
            base = step * 2 * GROUP
            pairs = [
                jnp.concatenate([held[base + 2 * q], held[base + 2 * q + 1]], 1)
                for q in range(GROUP)
            ]
            first = dot(jnp.concatenate(pairs, 0), wide2[...]).astype(BF16)
            for q in range(GROUP):
                done = dot(left1, first[q * width : (q + 1) * width]).astype(BF16).astype(F32)
                for h in range(2):
                    start = (base + 2 * q + h) * PITCH
                    second[pl.ds(start, width), :] = done[:, h * width : (h + 1) * width]
        left = left_rows(me, left0, classes, rows)
        for step in range(steps):
            base = step * 2 * GROUP
            done = []
            for q in range(GROUP):
                halves = [
                    second[pl.ds(base + 2 * q + h, width, stride=PITCH), :].astype(BF16)
                    for h in range(2)
                ]
                done.append(dot(left, jnp.concatenate(halves, 1)))
            put_tiles(made, done, base, rows, width)
            part = pl.ds(base * rows, 2 * GROUP * rows)
            for index in range(count if stored else 0):
                sem = sems.at[steps + step * count + index]
                stores.append(
                    pltpu.make_async_copy(made[index].at[part], outs[index].at[part], sem)
                )
                stores[-1].start()
        for store in stores:
            store.wait()

    return pl.pallas_call(
        kernel,
        out_shape=[place(shape, BF16)] * count,
        in_specs=[IN_HBM, IN_VMEM],
        out_specs=[IN_HBM if stored else IN_VMEM] * count,
        scratch_shapes=[
            pltpu.VMEM(blocks.shape, BF16),
            pltpu.VMEM((width, width), F32),
            pltpu.VMEM((2 * width, 2 * width), BF16),
            pltpu.VMEM((width * PITCH + width, width), F32),
            pltpu.SemaphoreType.DMA((steps * (1 + count) + 1,)),
        ]
        + [pltpu.VMEM(shape, BF16)] * (count if stored else 0),
        compiler_params=pltpu.CompilerParams(vmem_limit_bytes=40 * 2**20),
        cost_estimate=pl.CostEstimate(flops=0, bytes_accessed=0, transcendentals=0),
        name="contract",
    )(in_hbm(blocks), in_vmem(factors))


def receive(d, message, src, out, sums, following):
    rows, ncount, width, _ = src.shape
    blocks = lax.axis_size("sink")
    operands = [in_vmem(message), in_vmem(src)]
    specs = [IN_VMEM, IN_VMEM]
    shapes = [
        pltpu.HBM((rows, blocks, width, width), BF16),
        pltpu.VMEM((blocks, ncount, width), F32),
    ]
    places = [IN_HBM, IN_VMEM]
    aliases = {}
    if out is not None:
        aliases.update({2: 0, 3: 1})
        operands += [in_hbm(out), in_vmem(sums)]
        specs += places
    if following is not None:
        aliases[len(operands)] = 2
        operands.append(in_hbm(following))
        specs.append(IN_HBM)
        shapes.append(pltpu.HBM(following.shape, following.dtype))
        places = places + [IN_HBM]

    def kernel(*refs):
        message, src = refs[:2]
        out, sums = refs[len(operands) : len(operands) + 2]
        wide, stage, sems = refs[-3:]
        if 3 in aliases:
            sums[...] = refs[3][...]
        index = lax.axis_index("sink") ^ d
        wide[pl.ds(0, rows * width), :] = message[...].astype(F32)
        stores = []
        for r in range(rows):
            stage[r] = wide[pl.ds(r, width, stride=rows), :].astype(BF16)
            stores.append(pltpu.make_async_copy(stage.at[r], out.at[r, index], sems.at[r]))
            stores[-1].start()
        for c in range(ncount):
            total = jnp.zeros((8, width), F32)
            for r in range(rows):
                product = stage[r].astype(F32) * src[r, c].astype(F32)
                total = total + jnp.sum(product.reshape(width // 8, 8, width), axis=0)
            sums[index, pl.ds(c, 1)] = jnp.sum(total, axis=0, keepdims=True)
        for store in stores:
            store.wait()

    results = pl.pallas_call(
        kernel,
        out_shape=shapes,
        in_specs=specs,
        out_specs=places,
        scratch_shapes=[
            pltpu.VMEM((rows * width + rows, width), F32),
            pltpu.VMEM((rows, width, width), BF16),
            pltpu.SemaphoreType.DMA((rows,)),
        ],
        input_output_aliases=aliases,
        cost_estimate=pl.CostEstimate(flops=0, bytes_accessed=0, transcendentals=0),
        name="receive",
    )(*operands)
    return results if following is not None else (*results, None)


def determinant(correlation, pairs, tsources):
    ncount = correlation.shape[-1]
    grid = correlation.reshape(tsources, -1, NMOM, ncount)
    momenta = jnp.arange(NMOM, dtype=jnp.int32)
    pick_first = (pairs[:, 0][:, None] == momenta[None, :]).astype(F32)
    pick_second = (pairs[:, 1][:, None] == momenta[None, :]).astype(F32)
    first_one = jnp.einsum("pm,stmc->stpc", pick_first, grid, precision=lax.Precision.HIGHEST)
    second_one = jnp.einsum("pm,stmc->stpc", pick_second, grid, precision=lax.Precision.HIGHEST)
    return first_one[..., 0] * second_one[..., 1] - first_one[..., 1] * second_one[..., 0]


def finish(sums, pairs):
    devices, _, width = sums.shape
    times = devices // NMOM

    def kernel(pairs, sums, out):
        row = jnp.sum(sums[...], axis=0)
        time = lax.broadcasted_iota(jnp.int32, (times, width), 0)
        lane = lax.broadcasted_iota(jnp.int32, (times, width), 1)
        columns = []
        for p in range(pairs.shape[1]):
            values = [
                jnp.sum(
                    jnp.where(lane == 2 * (NMOM * time + pairs[k, p]) + c, row, 0.0),
                    axis=1,
                    keepdims=True,
                )
                for k in range(2)
                for c in range(2)
            ]
            columns.append(values[0] * values[3] - values[1] * values[2])
        out[0] = jnp.concatenate(columns, 1)

    return pl.pallas_call(
        kernel,
        out_shape=jax.ShapeDtypeStruct((1, times, pairs.shape[0]), F32),
        in_specs=[IN_SMEM, IN_VMEM],
        out_specs=IN_VMEM,
        name="finish",
    )(pairs.T, sums)


def by_classes(blocks, peram, src_blocks, sink_spin, src_spin, pairs):
    devices = lax.axis_size("sink")
    rows, ncount, width, _ = src_blocks.shape

    def send(d, message):
        return lax.ppermute(message, "sink", [(i, i ^ d) for i in range(devices)])

    picked = pick(peram, sink_spin, src_spin)
    factors = lax.all_to_all(picked, "sink", split_axis=0, concat_axis=0, tiled=True)
    far = list(range(devices // 2, devices))
    near = list(range(devices // 2 - 1, 0, -1))
    far = [d for pair in zip(far[: len(far) // 2], far[len(far) // 2 :]) for d in pair]
    far[:2] = far[1::-1]
    sent = []
    for f, c in zip(far, near + [None]):
        sent += [f] if c is None else [f, c]
    early = contract(blocks, factors, sent[:AHEAD], pltpu.VMEM)
    come = {d: send(d, message) for d, message in zip(sent, early)}
    rest = sent[AHEAD:] + [0]
    messages = dict(zip(rest, contract(blocks, factors, rest, pltpu.HBM)))
    out, sums, _ = receive(0, messages[0], src_blocks, None, None, None)
    for step, d in enumerate(sent):
        ahead = sent[step + AHEAD] if step + AHEAD < len(sent) else None
        out, sums, following = receive(
            d,
            come[d],
            src_blocks,
            out,
            sums,
            None if ahead is None else messages[ahead],
        )
        if ahead is not None:
            come[ahead] = send(ahead, following)
    row = jnp.sum(sums, axis=-1).reshape(1, 1, devices * ncount)
    row = jnp.pad(row, ((0, 0), (0, 0), (0, width - devices * ncount)))
    rows_of_all = lax.all_to_all(
        jnp.broadcast_to(row, (devices, 1, width)), "sink", split_axis=0, concat_axis=0, tiled=True
    )
    return out, finish(rows_of_all, pairs)


def by_all_to_all(blocks, peram, src_blocks, sink_spin, src_spin, pairs):
    width = blocks.shape[1]
    tsources = src_spin.shape[0]
    devices = lax.axis_size("sink")
    position = lax.axis_index("sink")
    per_rows = peram.shape[0]
    own_source = (position * per_rows + jnp.arange(per_rows, dtype=jnp.int32)) // width
    target_time = jnp.arange(devices, dtype=jnp.int32) // NMOM
    codes = 4 * sink_spin[None, :, :] + src_spin[own_source][:, None, :]
    picked = peram[
        jnp.arange(per_rows, dtype=jnp.int32)[:, None, None], target_time[None, :, None], codes, :
    ]
    incoming = lax.all_to_all(picked, "sink", split_axis=1, concat_axis=0, tiled=True)
    factors = incoming.reshape(tsources, width, 3, width)

    def transform(source):
        first = dot(blocks.reshape(-1, width), factors[source, :, 2]).astype(BF16)
        second = jnp.einsum(
            "ijk,jJ->iJk",
            first.reshape(blocks.shape),
            factors[source, :, 1],
            preferred_element_type=F32,
        ).astype(BF16)
        return jnp.einsum(
            "iI,iJk->IJk", factors[source, :, 0], second, preferred_element_type=F32
        ).astype(BF16)

    sending = jnp.stack([transform(s) for s in range(tsources)])
    sending = sending.reshape(tsources * width, 1, width, width)
    regrouped = lax.all_to_all(sending, "sink", split_axis=0, concat_axis=1, tiled=True)
    out_rows = regrouped.shape[0]
    row_source = (position * out_rows + jnp.arange(out_rows, dtype=jnp.int32)) // width
    sums = jnp.einsum("rbjk,rcjk->rbc", regrouped, src_blocks, preferred_element_type=F32)
    selector = (row_source[:, None] == jnp.arange(tsources, dtype=jnp.int32)[None, :]).astype(F32)
    local = jnp.einsum("rs,rbc->sbc", selector, sums, precision=lax.Precision.HIGHEST)
    return regrouped, determinant(lax.psum(local, "sink"), pairs, tsources)


def body(blocks, peram, src_blocks, sink_spin, src_spin, pairs):
    devices = lax.axis_size("sink")
    small = devices == 16 and src_spin.shape[0] == 1 and src_blocks.shape[:2] == (8, 2)
    run = by_classes if small else by_all_to_all
    return run(blocks, peram, src_blocks, sink_spin, src_spin, pairs)


def solution(mesh):
    placed = (
        P(("groups", "sink"), None, None),
        P(("groups", "sink"), None, None, None),
        P(("groups", "sink"), None, None, None),
        P(),
        P(),
        P(),
    )
    return jax.shard_map(
        body,
        mesh=mesh,
        in_specs=placed,
        out_specs=(P(("groups", "sink"), None, None, None), P("groups", None, None)),
        check_vma=False,
    )
```
